128 devices in a mesh: gx: 4 (over x_lo, core), gy: 4 (over y), gz: 8 (over x_hi, z).
Axes of the slice: x: 4 (x_hi: 2, x_lo: 2; x = x_hi * 2 + x_lo), y: 4, z: 4, core: 2. Of those that a mesh axis runs over, the one named last changes fastest.
Arguments:
- sources: bfloat16 [16, 4194304], P(None, ('gx', 'gy', 'gz')), may hold values from -6 to 6
- in_slot: int32 [16384], P(('gx', 'gy', 'gz')), may hold values from 0 to 127, as said below
- interp: bfloat16 [16384, 64, 256], P(('gx', 'gy', 'gz')), may hold values from -0.375 to 0.375
- translate: bfloat16 [7, 16384, 64, 128], P(None, ('gx', 'gy', 'gz')), may hold values from -0.5 to 0.5
- evaluate: bfloat16 [16384, 64, 256], P(('gx', 'gy', 'gz')), may hold values from -0.75 to 0.75
- owner_slot: int32 [16384], P(('gx', 'gy', 'gz')), may hold values from 0 to 127, as said below
Outputs:
- targets: bfloat16 [16, 4194304], P(None, ('gx', 'gy', 'gz'))
The draws below stay inside these ranges and needn't reach their ends.
Inputs may be any that keep to these rules, and one draw needn't show every extreme that they name: `in_slot`: each aligned block of 128 entries is a permutation of 0 to 127. `owner_slot`: each aligned block of 128 entries is a permutation of 0 to 127.
All inputs are finite; a program needn't handle non-finite values.
Results may differ from the reference program's by a relative error of at most 0.015.
Values may be sent and summed in bfloat16 or wider, within the bound.
No kernel may reach another device: no remote copies, remote signals or barrier semaphores. Data moves between devices by JAX's collectives and lax.ppermute only.
A program may use at most 128 MiB of HBM per device.

```python
import jax
import jax.numpy as jnp

RANK = 64
SPAN = 256
RHS = 16
BOX_DEV = 128
LEVELS = 7
NBOX = 16384
NPTS = 4194304
N_GX = 4
N_GY = 4
N_GZ = 8


def block_perms(key):
    keys = jax.random.split(key, NBOX // BOX_DEV)
    perms = jax.vmap(lambda single: jax.random.permutation(single, BOX_DEV))(keys)
    return perms.reshape(-1).astype(jnp.int32)


def draw_in_slot(key, part):
    key = jax.random.fold_in(key, 11)
    return block_perms(key)


def draw_owner_slot(key, part):
    key = jax.random.fold_in(key, 23)
    return block_perms(key)


def steps_of(rng, extent, cuts, low, largest):
    loudness = 1.0
    for dim, parts in cuts:
        steps = jax.random.uniform(jax.random.fold_in(jax.random.fold_in(rng, 6), dim), (parts,), jnp.float32, low / len(cuts), largest / len(cuts))
        loudness = loudness * jnp.repeat(jnp.exp(steps), extent[dim] // parts).reshape((-1,) + (1,) * (len(extent) - 1 - dim))
    return loudness


def gaussian(own_key, dims, scale, bound, cuts=(), kind=jnp.bfloat16):
    level = steps_of(own_key, dims, cuts, -0.22, 0.18) if cuts else 1.0
    entries = jax.random.normal(own_key, dims, jnp.float32) * scale * level
    return jnp.minimum(jnp.maximum(entries, -bound), bound).astype(kind)


def setup_inputs(seed: int = 0) -> dict:
    arg_keys = jax.random.split(jax.random.key(seed), 7)
    sources = gaussian(arg_keys[0], (RHS, NPTS), 1.0, 6.0, ((1, 128),))
    in_slot = draw_in_slot(jax.random.fold_in(arg_keys[6], 71), 0)
    interp = gaussian(arg_keys[2], (NBOX, RANK, SPAN), SPAN ** -0.5, 0.375, ((0, 128),))
    translate = gaussian(arg_keys[3], (LEVELS, NBOX, RANK, 2 * RANK), (2 * RANK) ** -0.5, 0.5, ((1, 128),))
    evaluate = gaussian(arg_keys[4], (NBOX, RANK, SPAN), RANK ** -0.5, 0.75, ((0, 128),))
    owner_slot = draw_owner_slot(jax.random.fold_in(arg_keys[6], 71), 0)
    return {"sources": sources, "in_slot": in_slot, "interp": interp, "translate": translate, "evaluate": evaluate, "owner_slot": owner_slot}


def reference(sources, in_slot, interp, translate, evaluate, owner_slot):
    blocks = N_GX * N_GY * N_GZ
    spread = sources.reshape(RHS, NBOX, SPAN)
    base = (jnp.arange(NBOX, dtype=jnp.int32) // BOX_DEV) * BOX_DEV
    chosen = spread[:, base + in_slot.astype(jnp.int32), :]
    coeffs = jnp.einsum("bks,rbs->bkr", interp.astype(jnp.float32), chosen.astype(jnp.float32)).astype(jnp.bfloat16)
    for level_no in range(LEVELS):
        lower = 2 ** level_no
        shaped = coeffs.reshape(blocks // (2 * lower), 2, lower, BOX_DEV, RANK, RHS)
        partner = shaped[:, ::-1].reshape(NBOX, RANK, RHS)
        tables = translate[level_no].astype(jnp.float32)
        mixed = jnp.einsum("bkj,bjr->bkr", tables[:, :, :RANK], coeffs.astype(jnp.float32))
        mixed = mixed + jnp.einsum("bkj,bjr->bkr", tables[:, :, RANK:], partner.astype(jnp.float32))
        coeffs = mixed.astype(jnp.bfloat16)
    values = jnp.einsum("bks,bkr->rbs", evaluate.astype(jnp.float32), coeffs.astype(jnp.float32)).astype(jnp.bfloat16)
    owner_dev = jnp.arange(NBOX, dtype=jnp.int32) // BOX_DEV
    source_box = owner_slot.astype(jnp.int32) * blocks + owner_dev
    return values[:, source_box, :].reshape(RHS, NPTS)
```

```python
import functools

import jax
import jax.numpy as jnp
from jax import lax
from jax.experimental import pallas as pl
from jax.experimental.pallas import tpu as pltpu
from jax.sharding import PartitionSpec as P

AXES = ("gx", "gy", "gz")
PACK = 8
CHUNKS = (8, 8)


def own_lanes(shape, cols):
    return lax.broadcasted_iota(jnp.int32, shape, 1) // cols


def pick(wide, rank, cols):
    lane_box = own_lanes((rank, PACK * cols), cols)
    out = wide[:rank]
    for box in range(1, PACK):
        out = jnp.where(lane_box == box, wide[box * rank : (box + 1) * rank], out)
    return out


def interp_body(first, per_step, slot_ref, src_ref, interp_ref, *rest):
    out_ref = rest[-1]
    _, rank, span = interp_ref.shape
    rhs = src_ref.shape[0]
    for grp in range(per_step):
        base = (first + pl.program_id(0) * per_step + grp) * PACK
        slabs = []
        for box in range(PACK):
            at = pl.multiple_of(slot_ref[base + box] * span, span)
            slabs.append(src_ref[:, pl.ds(at, span)])
        points = jnp.concatenate(slabs, axis=0)
        block = interp_ref[grp * PACK : (grp + 1) * PACK].reshape(PACK * rank, span)
        wide = lax.dot_general(
            block, points, (((1,), (1,)), ((), ())), preferred_element_type=jnp.float32
        )
        out_ref[grp] = pick(wide, rank, rhs).astype(jnp.bfloat16)


def interp_call(first, groups, slot, src, interp, *after):
    per_step = 2
    boxes, rank, span = interp.shape
    rhs = src.shape[0]
    lanes = PACK * rhs
    return pl.pallas_call(
        functools.partial(interp_body, first, per_step),
        grid_spec=pltpu.PrefetchScalarGridSpec(
            num_scalar_prefetch=1,
            grid=(groups // per_step,),
            in_specs=[
                pl.BlockSpec(src.shape, lambda i, s: (0, 0)),
                pl.BlockSpec(
                    (per_step * PACK, rank, span), lambda i, s: (first // per_step + i, 0, 0)
                ),
            ]
            + [pl.BlockSpec(memory_space=pl.ANY)] * len(after),
            out_specs=pl.BlockSpec((per_step, rank, lanes), lambda i, s: (i, 0, 0)),
        ),
        out_shape=jax.ShapeDtypeStruct((groups, rank, lanes), jnp.bfloat16),
        compiler_params=pltpu.CompilerParams(vmem_limit_bytes=24 * 2**20),
        cost_estimate=pl.CostEstimate(
            flops=2 * groups * lanes * rank * span,
            bytes_accessed=groups * PACK * rank * span * 2 + src.size * 2,
            transcendentals=0,
        ),
        name="interp",
    )(slot, src, interp, *after)


def level_body(per_step, table_ref, own_ref, far_ref, *rest):
    out_ref = rest[-1]
    _, _, rank, both = table_ref.shape
    lanes = own_ref.shape[2]
    for grp in range(per_step):
        block = table_ref[0, grp * PACK : (grp + 1) * PACK].reshape(PACK * rank, both)
        pair = jnp.concatenate([own_ref[grp], far_ref[grp]], axis=0)
        wide = jnp.dot(block, pair, preferred_element_type=jnp.float32)
        out_ref[grp] = pick(wide, rank, lanes // PACK).astype(jnp.bfloat16)


def level_call(level, first, tables, own, far, *after):
    per_step = 2
    groups, rank, lanes = own.shape
    both = tables.shape[3]
    return pl.pallas_call(
        functools.partial(level_body, per_step),
        grid=(groups // per_step,),
        in_specs=[
            pl.BlockSpec(
                (1, per_step * PACK, rank, both), lambda i: (level, first // per_step + i, 0, 0)
            ),
            pl.BlockSpec((per_step, rank, lanes), lambda i: (i, 0, 0)),
            pl.BlockSpec((per_step, rank, lanes), lambda i: (i, 0, 0)),
        ]
        + [pl.BlockSpec(memory_space=pl.ANY)] * len(after),
        out_specs=pl.BlockSpec((per_step, rank, lanes), lambda i: (i, 0, 0)),
        out_shape=jax.ShapeDtypeStruct(own.shape, jnp.bfloat16),
        compiler_params=pltpu.CompilerParams(vmem_limit_bytes=24 * 2**20),
        cost_estimate=pl.CostEstimate(
            flops=2 * groups * lanes * rank * both,
            bytes_accessed=groups * PACK * rank * both * 2,
            transcendentals=0,
        ),
        name="level",
    )(tables, own, far, *after)


def eval_body(per_step, coeffs_ref, eval_ref, *rest):
    out_ref = rest[-1]
    _, rank, span = eval_ref.shape
    lanes = coeffs_ref.shape[2]
    rhs = lanes // PACK
    for grp in range(per_step):
        mine = coeffs_ref[grp].astype(jnp.float32)
        twice = jnp.concatenate([mine, mine], axis=0).T.astype(jnp.bfloat16)
        left = jnp.concatenate([twice] * (PACK // 2), axis=1)
        row_box = lax.broadcasted_iota(jnp.int32, left.shape, 0) // rhs
        col_box = lax.broadcasted_iota(jnp.int32, left.shape, 1) // rank
        left = jnp.where(row_box == col_box, left, jnp.zeros_like(left))
        block = eval_ref[grp * PACK : (grp + 1) * PACK].reshape(PACK * rank, span)
        vals = jnp.dot(left, block, preferred_element_type=jnp.float32)
        out_ref[grp * PACK : (grp + 1) * PACK] = vals.astype(jnp.bfloat16).reshape(
            PACK, rhs, span
        )


def eval_call(first, coeffs, evaluate, *before):
    per_step = 2
    groups, rank, lanes = coeffs.shape
    boxes, _, span = evaluate.shape
    rhs = lanes // PACK
    return pl.pallas_call(
        functools.partial(eval_body, per_step),
        grid=(groups // per_step,),
        in_specs=[
            pl.BlockSpec((per_step, rank, lanes), lambda i: (i, 0, 0)),
            pl.BlockSpec((per_step * PACK, rank, span), lambda i: (first // per_step + i, 0, 0)),
        ]
        + [pl.BlockSpec(memory_space=pl.ANY)] * len(before),
        out_specs=pl.BlockSpec(
            (per_step * PACK, rhs, span), lambda i: (first // per_step + i, 0, 0)
        ),
        out_shape=jax.ShapeDtypeStruct((boxes, rhs, span), jnp.bfloat16),
        input_output_aliases={2: 0} if before else {},
        compiler_params=pltpu.CompilerParams(vmem_limit_bytes=24 * 2**20),
        cost_estimate=pl.CostEstimate(
            flops=2 * groups * lanes * rank * span,
            bytes_accessed=groups * PACK * (rank + rhs) * span * 2,
            transcendentals=0,
        ),
        name="evaluate",
    )(coeffs, evaluate, *before)


def place_body(per_step, slot_ref, got_ref, out_ref):
    span = got_ref.shape[2]
    base = pl.program_id(0) * per_step
    for box in range(per_step):
        out_ref[:, box * span : (box + 1) * span] = got_ref[slot_ref[base + box]]


def place_call(slot, got):
    per_step = 32
    boxes, rhs, span = got.shape
    return pl.pallas_call(
        functools.partial(place_body, per_step),
        grid_spec=pltpu.PrefetchScalarGridSpec(
            num_scalar_prefetch=1,
            grid=(boxes // per_step,),
            in_specs=[pl.BlockSpec(got.shape, lambda i, s: (0, 0, 0))],
            out_specs=pl.BlockSpec((rhs, per_step * span), lambda i, s: (0, i)),
        ),
        out_shape=jax.ShapeDtypeStruct((rhs, boxes * span), got.dtype),
        compiler_params=pltpu.CompilerParams(vmem_limit_bytes=24 * 2**20),
        cost_estimate=pl.CostEstimate(
            flops=0, bytes_accessed=4 * got.size, transcendentals=0
        ),
        name="place",
    )(slot, got)


def from_partner(value, axis, distance):
    mask = 2**distance
    pairs = [(source, source ^ mask) for source in range(lax.axis_size(axis))]
    return lax.ppermute(value, axis, pairs)


def local(sources, in_slot, interp, translate, evaluate, owner_slot):
    firsts = [sum(CHUNKS[:i]) for i in range(len(CHUNKS))]
    coeffs = []
    for first, groups in zip(firsts, CHUNKS):
        coeffs.append(interp_call(first, groups, in_slot, sources, interp, *coeffs[-1:]))
    steps = [
        (axis, bit_pos)
        for axis in ("gz", "gy", "gx")
        for bit_pos in range(lax.axis_size(axis).bit_length() - 1)
    ]
    for level, (axis, bit_pos) in enumerate(steps):
        last = coeffs[-1]
        for i, first in enumerate(firsts):
            far = from_partner(coeffs[i], axis, bit_pos)
            after = () if len(firsts) == 1 else (last,)
            last = coeffs[i] = level_call(level, first, translate, coeffs[i], far, *after)
    values = ()
    for i, first in enumerate(firsts):
        values = (eval_call(first, coeffs[i], evaluate, *values),)
    moved = lax.all_to_all(values[0], AXES, split_axis=0, concat_axis=0, tiled=True)
    return place_call(owner_slot, moved)


def solution(mesh):
    placed = (
        P(None, AXES),
        P(AXES),
        P(AXES, None, None),
        P(None, AXES, None, None),
        P(AXES, None, None),
        P(AXES),
    )
    return jax.shard_map(
        local, mesh=mesh, in_specs=placed, out_specs=P(None, AXES), check_vma=False
    )
```

```python
import functools

import jax
import jax.numpy as jnp
from jax import lax
from jax.experimental import pallas as pl
from jax.experimental.pallas import tpu as pltpu
from jax.sharding import PartitionSpec as P

AXES = ("gx", "gy", "gz")
PACK = 8
CHUNKS = (8, 8)
KEEP = True
LOADS = (2, 2, 3)
VMEM_LIMIT = 16 * 2**20
INTERP_LIMITS = (53.25, 53.25)
LOAD_LIMITS = (40, 38, 36)
MIB = 2**20


def own_lanes(shape, cols):
    return lax.broadcasted_iota(jnp.int32, shape, 1) // cols


def pick(wide, rank, cols):
    lane_box = own_lanes((rank, PACK * cols), cols)
    out = wide[:rank]
    for box in range(1, PACK):
        out = jnp.where(lane_box == box, wide[box * rank : (box + 1) * rank], out)
    return out


def interp_body(first, groups, pieces, slot_hbm, src_hbm, interp_hbm, *rest):
    out_ref, slot_ref, src_ref, interp_ref, sems = rest[-5:]
    _, rank, span = interp_ref.shape
    rhs = src_ref.shape[0]
    per = groups // pieces
    slot_load = pltpu.make_async_copy(slot_hbm, slot_ref, sems.at[pieces + 1])
    slot_load.start()
    load = pltpu.make_async_copy(src_hbm, src_ref, sems.at[pieces])
    load.start()
    loads = []
    for piece in range(pieces):
        at = pl.ds(piece * per * PACK, per * PACK)
        loads.append(
            pltpu.make_async_copy(
                interp_hbm.at[pl.ds(first * PACK + piece * per * PACK, per * PACK)],
                interp_ref.at[at],
                sems.at[piece],
            )
        )
        loads[-1].start()
    slot_load.wait()
    load.wait()
    for grp in range(groups):
        if grp % per == 0:
            loads[grp // per].wait()
        slabs = []
        for box in range(PACK):
            at = pl.multiple_of(slot_ref[(first + grp) * PACK + box] * span, span)
            slabs.append(src_ref[:, pl.ds(at, span)])
        points = jnp.concatenate(slabs, axis=0)
        block = interp_ref[grp * PACK : (grp + 1) * PACK].reshape(PACK * rank, span)
        wide = lax.dot_general(
            block, points, (((1,), (1,)), ((), ())), preferred_element_type=jnp.float32
        )
        out_ref[grp] = pick(wide, rank, rhs).astype(jnp.bfloat16)


def interp_call(limit, first, groups, slot, src, interp, *after):
    pieces = 4
    _, rank, span = interp.shape
    lanes = PACK * src.shape[0]
    return pl.pallas_call(
        functools.partial(interp_body, first, groups, pieces),
        in_specs=[pl.BlockSpec(memory_space=pl.ANY)] * (3 + len(after)),
        out_specs=pl.BlockSpec(memory_space=pltpu.VMEM),
        out_shape=jax.ShapeDtypeStruct((groups, rank, lanes), jnp.bfloat16),
        scratch_shapes=[
            pltpu.SMEM(slot.shape, slot.dtype),
            pltpu.VMEM(src.shape, src.dtype),
            pltpu.VMEM((groups * PACK, rank, span), interp.dtype),
            pltpu.SemaphoreType.DMA((pieces + 2,)),
        ],
        compiler_params=pltpu.CompilerParams(vmem_limit_bytes=int(limit * MIB)),
        cost_estimate=pl.CostEstimate(
            flops=2 * groups * lanes * rank * span,
            bytes_accessed=groups * PACK * rank * span * 2 + src.size * 2,
            transcendentals=0,
        ),
        name="interp",
    )(slot, src, interp, *after)


def load_body(levels, table_hbm, *rest):
    sems = rest[-1]
    loads = []
    for i, level in enumerate(levels):
        loads.append(pltpu.make_async_copy(table_hbm.at[level], rest[-1 - len(levels) + i], sems.at[i]))
        loads[-1].start()
    for load in loads:
        load.wait()


def load_call(limit, levels, tables, *after):
    shape = tables.shape[1:]
    return pl.pallas_call(
        functools.partial(load_body, levels),
        in_specs=[pl.BlockSpec(memory_space=pl.ANY)] * (1 + len(after)),
        out_specs=[pl.BlockSpec(memory_space=pltpu.VMEM)] * len(levels),
        out_shape=[jax.ShapeDtypeStruct(shape, tables.dtype)] * len(levels),
        scratch_shapes=[pltpu.SemaphoreType.DMA((len(levels),))],
        compiler_params=pltpu.CompilerParams(vmem_limit_bytes=int(limit * MIB)),
        cost_estimate=pl.CostEstimate(
            flops=0,
            bytes_accessed=len(levels) * shape[0] * shape[1] * shape[2] * 2,
            transcendentals=0,
        ),
        name="load",
    )(tables, *after)


def level_body(first, table_ref, own_ref, far_ref, *rest):
    out_ref = rest[-1]
    _, rank, both = table_ref.shape
    groups, _, lanes = own_ref.shape
    for grp in range(groups):
        at = (first + grp) * PACK
        block = table_ref[at : at + PACK].reshape(PACK * rank, both)
        pair = jnp.concatenate([own_ref[grp], far_ref[grp]], axis=0)
        wide = jnp.dot(block, pair, preferred_element_type=jnp.float32)
        out_ref[grp] = pick(wide, rank, lanes // PACK).astype(jnp.bfloat16)


def level_call(first, table, own, far, *after):
    groups, rank, lanes = own.shape
    both = table.shape[2]
    return pl.pallas_call(
        functools.partial(level_body, first),
        in_specs=[pl.BlockSpec(memory_space=pltpu.VMEM)] * 3
        + [pl.BlockSpec(memory_space=pl.ANY)] * len(after),
        out_specs=pl.BlockSpec(memory_space=pltpu.VMEM),
        out_shape=jax.ShapeDtypeStruct(own.shape, jnp.bfloat16),
        compiler_params=pltpu.CompilerParams(vmem_limit_bytes=VMEM_LIMIT),
        cost_estimate=pl.CostEstimate(
            flops=2 * groups * lanes * rank * both,
            bytes_accessed=groups * PACK * rank * both * 2,
            transcendentals=0,
        ),
        name="level",
    )(table, own, far, *after)


def eval_body(first, coeffs_ref, eval_ref, *rest):
    out_ref = rest[-1]
    _, rank, span = eval_ref.shape
    groups, _, lanes = coeffs_ref.shape
    rhs = lanes // PACK
    for grp in range(groups):
        mine = coeffs_ref[grp].astype(jnp.float32)
        twice = jnp.concatenate([mine, mine], axis=0).T.astype(jnp.bfloat16)
        left = jnp.concatenate([twice] * (PACK // 2), axis=1)
        row_box = lax.broadcasted_iota(jnp.int32, left.shape, 0) // rhs
        col_box = lax.broadcasted_iota(jnp.int32, left.shape, 1) // rank
        left = jnp.where(row_box == col_box, left, jnp.zeros_like(left))
        at = (first + grp) * PACK
        block = eval_ref[at : at + PACK].reshape(PACK * rank, span)
        vals = jnp.dot(left, block, preferred_element_type=jnp.float32)
        out_ref[at : at + PACK] = vals.astype(jnp.bfloat16).reshape(PACK, rhs, span)


def eval_call(first, coeffs, evaluate, *before):
    groups, rank, lanes = coeffs.shape
    boxes, _, span = evaluate.shape
    rhs = lanes // PACK
    return pl.pallas_call(
        functools.partial(eval_body, first),
        in_specs=[pl.BlockSpec(memory_space=pltpu.VMEM)] * (2 + len(before)),
        out_specs=pl.BlockSpec(memory_space=pltpu.VMEM),
        out_shape=jax.ShapeDtypeStruct((boxes, rhs, span), jnp.bfloat16),
        input_output_aliases={2: 0} if before else {},
        compiler_params=pltpu.CompilerParams(vmem_limit_bytes=VMEM_LIMIT),
        cost_estimate=pl.CostEstimate(
            flops=2 * groups * lanes * rank * span,
            bytes_accessed=groups * PACK * (rank + rhs) * span * 2,
            transcendentals=0,
        ),
        name="evaluate",
    )(coeffs, evaluate, *before)


def place_body(pieces, slot_ref, got_ref, *rest):
    out_hbm, out_ref, sems = rest[-3:]
    boxes, _, span = got_ref.shape
    per = boxes // pieces
    stores = []
    for piece in range(pieces):
        for box in range(piece * per, (piece + 1) * per):
            out_ref[:, box * span : (box + 1) * span] = got_ref[slot_ref[box]]
        at = pl.ds(piece * per * span, per * span)
        stores.append(
            pltpu.make_async_copy(out_ref.at[:, at], out_hbm.at[:, at], sems.at[piece])
        )
        stores[-1].start()
    for store in stores:
        store.wait()


def place_call(slot, got, *kept):
    pieces = 4
    boxes, rhs, span = got.shape
    shape = (rhs, boxes * span)
    return pl.pallas_call(
        functools.partial(place_body, pieces),
        in_specs=[
            pl.BlockSpec(memory_space=pltpu.SMEM),
            pl.BlockSpec(memory_space=pltpu.VMEM),
        ]
        + [pl.BlockSpec(memory_space=pl.ANY)] * len(kept),
        out_specs=pl.BlockSpec(memory_space=pl.ANY),
        out_shape=jax.ShapeDtypeStruct(shape, got.dtype),
        scratch_shapes=[
            pltpu.VMEM(shape, got.dtype),
            pltpu.SemaphoreType.DMA((pieces,)),
        ],
        compiler_params=pltpu.CompilerParams(vmem_limit_bytes=VMEM_LIMIT),
        cost_estimate=pl.CostEstimate(
            flops=0, bytes_accessed=4 * got.size, transcendentals=0
        ),
        name="place",
    )(slot, got, *kept)


def from_partner(value, axis, distance):
    mask = 2**distance
    pairs = [(source, source ^ mask) for source in range(lax.axis_size(axis))]
    return lax.ppermute(value, axis, pairs)


def local(sources, in_slot, interp, translate, evaluate, owner_slot):
    firsts = [sum(CHUNKS[:i]) for i in range(len(CHUNKS))]
    coeffs = []
    for limit, first, groups in zip(INTERP_LIMITS, firsts, CHUNKS):
        coeffs.append(interp_call(limit, first, groups, in_slot, sources, interp, *coeffs[-1:]))
    steps = [
        (axis, bit_pos)
        for axis in ("gz", "gy", "gx")
        for bit_pos in range(lax.axis_size(axis).bit_length() - 1)
    ]
    kept, held = [], []
    for level, (axis, bit_pos) in enumerate(steps):
        last = coeffs[-1]
        if level < len(LOADS):
            levels = range(len(held), len(held) + LOADS[level])
            held += load_call(LOAD_LIMITS[level], levels, translate, last)
        for i, first in enumerate(firsts):
            far = from_partner(coeffs[i], axis, bit_pos)
            kept += [coeffs[i], far]
            after = () if len(firsts) == 1 else (last,)
            last = coeffs[i] = level_call(first, held[level], coeffs[i], far, *after)
    values = ()
    for i, first in enumerate(firsts):
        values = (eval_call(first, coeffs[i], evaluate, *values),)
    moved = lax.all_to_all(values[0], AXES, split_axis=0, concat_axis=0, tiled=True)
    return place_call(owner_slot, moved, *(kept if KEEP else ()))


def solution(mesh):
    placed = (
        P(None, AXES),
        P(AXES),
        P(AXES, None, None),
        P(None, AXES, None, None),
        P(AXES, None, None),
        P(AXES),
    )
    return jax.shard_map(
        local, mesh=mesh, in_specs=placed, out_specs=P(None, AXES), check_vma=False
    )
```

```python
import functools
import itertools

import jax
import jax.numpy as jnp
import numpy as np
from jax import lax
from jax.experimental import pallas as pl
from jax.experimental.pallas import tpu as pltpu
from jax.sharding import PartitionSpec as P

AXES = ("gx", "gy", "gz")
PACK = 8
CHUNKS = (8, 8)
LOADS = {0: 2, 1: 1, 2: 1, 3: 2, 6: 1}
PIECES = 4
ORDER = (1, 2, 3, 0, 4)
SPLIT = (2, 2, 4, 2, 4)
MIB = 2**20
FREE = pl.CostEstimate(flops=0, bytes_accessed=0, transcendentals=0)
VMEM_LIMIT = 16 * MIB
INTERP_LIMIT = int(53.25 * MIB)
LOAD_LIMIT = 38 * MIB


def own_lanes(shape, cols):
    return lax.broadcasted_iota(jnp.int32, shape, 1) // cols


def pick(wide, rank, cols):
    lane_box = own_lanes((rank, PACK * cols), cols)
    out = wide[:rank]
    for box in range(1, PACK):
        out = jnp.where(lane_box == box, wide[box * rank : (box + 1) * rank], out)
    return out


def interp_body(firsts, slot_hbm, src_hbm, interp_hbm, *rest):
    *out_refs, slot_ref, src_ref, interp_ref, sems = rest
    boxes, rank, span = interp_ref.shape
    rhs = src_ref.shape[0]
    per = boxes // PIECES
    ready = [
        pltpu.make_async_copy(slot_hbm, slot_ref, sems.at[0]),
        pltpu.make_async_copy(src_hbm, src_ref, sems.at[1]),
    ]
    loads = []
    for piece in range(PIECES):
        at = pl.ds(piece * per, per)
        loads.append(
            pltpu.make_async_copy(interp_hbm.at[at], interp_ref.at[at], sems.at[2 + piece])
        )
    for copy in ready + loads:
        copy.start()
    for copy in ready:
        copy.wait()
    for first, out_ref in zip(firsts, out_refs):
        for grp in range(out_ref.shape[0]):
            base = (first + grp) * PACK
            slabs = []
            for box in range(PACK):
                at = pl.multiple_of(slot_ref[base + box] * span, span)
                slabs.append(src_ref[:, pl.ds(at, span)])
            inputs = jnp.concatenate(slabs, axis=0)
            if base % per == 0:
                loads[base // per].wait()
            block = interp_ref[base : base + PACK].reshape(PACK * rank, span)
            wide = lax.dot_general(
                block, inputs, (((1,), (1,)), ((), ())), preferred_element_type=jnp.float32
            )
            out_ref[grp] = pick(wide, rank, rhs).astype(jnp.bfloat16)


def interp_call(firsts, slot, src, interp):
    _, rank, span = interp.shape
    lanes = PACK * src.shape[0]
    return pl.pallas_call(
        functools.partial(interp_body, firsts),
        in_specs=[pl.BlockSpec(memory_space=pl.ANY)] * 3,
        out_specs=[pl.BlockSpec(memory_space=pltpu.VMEM)] * len(firsts),
        out_shape=[
            jax.ShapeDtypeStruct((groups, rank, lanes), jnp.bfloat16) for groups in CHUNKS
        ],
        scratch_shapes=[
            pltpu.SMEM(slot.shape, slot.dtype),
            pltpu.VMEM(src.shape, src.dtype),
            pltpu.VMEM(interp.shape, interp.dtype),
            pltpu.SemaphoreType.DMA((2 + PIECES,)),
        ],
        compiler_params=pltpu.CompilerParams(vmem_limit_bytes=INTERP_LIMIT),
        cost_estimate=FREE,
        name="interp",
    )(slot, src, interp)


def load_body(levels, whole, table_hbm, *rest):
    sems = rest[-1]
    loaded = rest[whole + 1 : -1]
    sources = [table_hbm.at[level] for level in levels] + list(rest[:whole])
    loads = [
        pltpu.make_async_copy(source, target, sems.at[i])
        for i, (source, target) in enumerate(zip(sources, loaded))
    ]
    for copy in loads:
        copy.start()
    for copy in loads:
        copy.wait()


def load_call(levels, tables, whole, after):
    outs = [jax.ShapeDtypeStruct(tables.shape[1:], tables.dtype)] * len(levels)
    outs += [jax.ShapeDtypeStruct(array.shape, array.dtype) for array in whole]
    return pl.pallas_call(
        functools.partial(load_body, levels, len(whole)),
        in_specs=[pl.BlockSpec(memory_space=pl.ANY)] * (2 + len(whole)),
        out_specs=[pl.BlockSpec(memory_space=pltpu.VMEM)] * len(outs),
        out_shape=outs,
        scratch_shapes=[pltpu.SemaphoreType.DMA((len(outs),))],
        compiler_params=pltpu.CompilerParams(vmem_limit_bytes=LOAD_LIMIT),
        cost_estimate=FREE,
        name="load",
    )(tables, *whole, after)


def level_body(first, table_ref, own_ref, far_ref, *rest):
    out_ref = rest[-1]
    _, rank, both = table_ref.shape
    groups, _, lanes = own_ref.shape
    for grp in range(groups):
        at = (first + grp) * PACK
        block = table_ref[at : at + PACK].reshape(PACK * rank, both)
        pair = jnp.concatenate([own_ref[grp], far_ref[grp]], axis=0)
        wide = jnp.dot(block, pair, preferred_element_type=jnp.float32)
        out_ref[grp] = pick(wide, rank, lanes // PACK).astype(jnp.bfloat16)


def level_call(first, table, own, far, *after):
    groups, rank, lanes = own.shape
    both = table.shape[2]
    return pl.pallas_call(
        functools.partial(level_body, first),
        in_specs=[pl.BlockSpec(memory_space=pltpu.VMEM)] * 3
        + [pl.BlockSpec(memory_space=pl.ANY)] * len(after),
        out_specs=pl.BlockSpec(memory_space=pltpu.VMEM),
        out_shape=jax.ShapeDtypeStruct(own.shape, jnp.bfloat16),
        compiler_params=pltpu.CompilerParams(vmem_limit_bytes=VMEM_LIMIT),
        cost_estimate=FREE,
        name="level",
    )(table, own, far, *after)


def eval_body(first, place_of, coeffs_ref, eval_ref, *rest):
    out_ref = rest[-1]
    _, rank, span = eval_ref.shape
    groups, _, lanes = coeffs_ref.shape
    rhs = lanes // PACK
    for grp in range(groups):
        mine = coeffs_ref[grp].astype(jnp.float32)
        twice = jnp.concatenate([mine, mine], axis=0).T.astype(jnp.bfloat16)
        left = jnp.concatenate([twice] * (PACK // 2), axis=1)
        row_box = lax.broadcasted_iota(jnp.int32, left.shape, 0) // rhs
        col_box = lax.broadcasted_iota(jnp.int32, left.shape, 1) // rank
        left = jnp.where(row_box == col_box, left, jnp.zeros_like(left))
        at = (first + grp) * PACK
        block = eval_ref[at : at + PACK].reshape(PACK * rank, span)
        vals = jnp.dot(left, block, preferred_element_type=jnp.float32)
        for box in range(PACK):
            mine = vals[box * rhs : (box + 1) * rhs]
            out_ref[place_of[at + box]] = mine.astype(jnp.bfloat16)


def eval_call(first, place_of, coeffs, evaluate, *before):
    groups, rank, lanes = coeffs.shape
    boxes, _, span = evaluate.shape
    rhs = lanes // PACK
    return pl.pallas_call(
        functools.partial(eval_body, first, place_of),
        in_specs=[pl.BlockSpec(memory_space=pltpu.VMEM)] * (2 + len(before)),
        out_specs=pl.BlockSpec(memory_space=pltpu.VMEM),
        out_shape=jax.ShapeDtypeStruct((boxes, rhs, span), jnp.bfloat16),
        input_output_aliases={2: 0} if before else {},
        compiler_params=pltpu.CompilerParams(vmem_limit_bytes=VMEM_LIMIT),
        cost_estimate=FREE,
        name="evaluate",
    )(coeffs, evaluate, *before)


def bits_by_shift():
    widths = [size.bit_length() - 1 for size in SPLIT]
    old = {axis: sum(widths[axis + 1 :]) for axis in range(len(SPLIT))}
    masks = {}
    for at, axis in enumerate(ORDER):
        new = sum(widths[later] for later in ORDER[at + 1 :])
        shift = new - old[axis]
        masks[shift] = masks.get(shift, 0) | (SPLIT[axis] - 1) << new
    return sorted(masks.items())


def place_of_device(device):
    place = 0
    for shift, mask in bits_by_shift():
        moved = device << shift if shift >= 0 else device >> -shift
        place = place | (moved & mask)
    return place


def place_body(pieces, slot_ref, got_ref, *rest):
    out_hbm, out_ref, sems = rest[-3:]
    boxes, _, span = got_ref.shape
    per = boxes // pieces
    stores = []
    for piece in range(pieces):
        for box in range(piece * per, (piece + 1) * per):
            out_ref[:, box * span : (box + 1) * span] = got_ref[place_of_device(slot_ref[box])]
        at = pl.ds(piece * per * span, per * span)
        stores.append(
            pltpu.make_async_copy(out_ref.at[:, at], out_hbm.at[:, at], sems.at[piece])
        )
        stores[-1].start()
    for store in stores:
        store.wait()


def place_call(slot, got):
    pieces = 4
    boxes, rhs, span = got.shape
    shape = (rhs, boxes * span)
    return pl.pallas_call(
        functools.partial(place_body, pieces),
        in_specs=[
            pl.BlockSpec(memory_space=pltpu.SMEM),
            pl.BlockSpec(memory_space=pltpu.VMEM),
        ],
        out_specs=pl.BlockSpec(memory_space=pl.ANY),
        out_shape=jax.ShapeDtypeStruct(shape, got.dtype),
        scratch_shapes=[
            pltpu.VMEM(shape, got.dtype),
            pltpu.SemaphoreType.DMA((pieces,)),
        ],
        compiler_params=pltpu.CompilerParams(vmem_limit_bytes=VMEM_LIMIT),
        cost_estimate=FREE,
        name="place",
    )(slot, got)


def from_partner(value, axis, distance):
    mask = 2**distance
    pairs = [(source, source ^ mask) for source in range(lax.axis_size(axis))]
    return lax.ppermute(value, axis, pairs)


def local(sources, in_slot, interp, translate, evaluate, owner_slot):
    firsts = [sum(CHUNKS[:i]) for i in range(len(CHUNKS))]
    coeffs = list(interp_call(firsts, in_slot, sources, interp))
    held = []
    steps = [
        (axis, bit_pos)
        for axis in ("gz", "gy", "gx")
        for bit_pos in range(lax.axis_size(axis).bit_length() - 1)
    ]
    tables = {}
    last = coeffs[-1]
    for level, i in itertools.product(range(len(steps)), range(len(firsts))):
        axis, bit_pos = steps[level]
        if i == 0:
            more = ()
            if level in LOADS:
                levels = range(len(held), len(held) + LOADS[level])
                final = level == len(steps) - 1
                more = load_call(levels, translate, [evaluate] * final, coeffs[-1])
                held += more[: len(levels)]
                if final:
                    evaluate = more[-1]
            tables[level] = more[:1]
        far = from_partner(coeffs[i], axis, bit_pos)
        last = coeffs[i] = level_call(
            firsts[i], held[level], coeffs[i], far, last, *tables[level]
        )
    devices = np.arange(int(np.prod(SPLIT))).reshape(SPLIT).transpose(ORDER).reshape(-1)
    group = [int(device) for device in devices]
    place_of = [int(at) for at in np.argsort(devices)]
    values = ()
    for i, first in enumerate(firsts):
        values = (eval_call(first, place_of, coeffs[i], evaluate, *values),)
    moved = lax.all_to_all(
        values[0], AXES, split_axis=0, concat_axis=0, axis_index_groups=[group], tiled=True
    )
    return place_call(owner_slot, moved)


def solution(mesh):
    placed = (
        P(None, AXES),
        P(AXES),
        P(AXES, None, None),
        P(None, AXES, None, None),
        P(AXES, None, None),
        P(AXES),
    )
    return jax.shard_map(
        local, mesh=mesh, in_specs=placed, out_specs=P(None, AXES), check_vma=False
    )
```

```python
import functools

import jax
import jax.numpy as jnp
import numpy as np
from jax import lax
from jax.experimental import pallas as pl
from jax.experimental.pallas import tpu as pltpu
from jax.sharding import PartitionSpec as P

AXES = ("gx", "gy", "gz")
PACK = 8
CHUNKS = (8, 8)
EARLY = 1
LOADS = {0: 1, 1: 1, 2: 1, 3: 2, 6: 1}
PIECES = 4
ORDER = (1, 2, 3, 0, 4)
SPLIT = (2, 2, 4, 2, 4)
CORE_STEP = ("gx", 0)
CORE_PARTS = 2
EVALUATE_COST = pl.CostEstimate(flops=10**9, bytes_accessed=0, transcendentals=0)
MIB = 2**20
FREE = pl.CostEstimate(flops=0, bytes_accessed=0, transcendentals=0)
VMEM_LIMIT = 16 * MIB
INTERP_LIMIT = int(53.25 * MIB)
LOAD_LIMIT = 38 * MIB


def own_lanes(shape, cols):
    return lax.broadcasted_iota(jnp.int32, shape, 1) // cols


def pick(wide, rank, cols):
    lane_box = own_lanes((rank, PACK * cols), cols)
    out = wide[:rank]
    for box in range(1, PACK):
        out = jnp.where(lane_box == box, wide[box * rank : (box + 1) * rank], out)
    return out


def interp_body(firsts, slot_hbm, src_hbm, interp_hbm, *rest):
    *out_refs, slot_ref, src_ref, interp_ref, sems = rest
    boxes, rank, span = interp_ref.shape
    rhs = src_ref.shape[0]
    per = boxes // PIECES
    ready = [
        pltpu.make_async_copy(slot_hbm, slot_ref, sems.at[0]),
        pltpu.make_async_copy(src_hbm, src_ref, sems.at[1]),
    ]
    loads = []
    for piece in range(PIECES):
        at = pl.ds(piece * per, per)
        loads.append(
            pltpu.make_async_copy(interp_hbm.at[at], interp_ref.at[at], sems.at[2 + piece])
        )
    for copy in ready + loads:
        copy.start()
    for copy in ready:
        copy.wait()
    for first, out_ref in zip(firsts, out_refs):
        for grp in range(out_ref.shape[0]):
            base = (first + grp) * PACK
            slabs = []
            for box in range(PACK):
                at = pl.multiple_of(slot_ref[base + box] * span, span)
                slabs.append(src_ref[:, pl.ds(at, span)])
            inputs = jnp.concatenate(slabs, axis=0)
            if base % per == 0:
                loads[base // per].wait()
            block = interp_ref[base : base + PACK].reshape(PACK * rank, span)
            wide = lax.dot_general(
                block, inputs, (((1,), (1,)), ((), ())), preferred_element_type=jnp.float32
            )
            out_ref[grp] = pick(wide, rank, rhs).astype(jnp.bfloat16)


def interp_call(firsts, slot, src, interp):
    _, rank, span = interp.shape
    lanes = PACK * src.shape[0]
    return pl.pallas_call(
        functools.partial(interp_body, firsts),
        in_specs=[pl.BlockSpec(memory_space=pl.ANY)] * 3,
        out_specs=[pl.BlockSpec(memory_space=pltpu.VMEM)] * len(firsts),
        out_shape=[
            jax.ShapeDtypeStruct((groups, rank, lanes), jnp.bfloat16) for groups in CHUNKS
        ],
        scratch_shapes=[
            pltpu.SMEM(slot.shape, slot.dtype),
            pltpu.VMEM(src.shape, src.dtype),
            pltpu.VMEM(interp.shape, interp.dtype),
            pltpu.SemaphoreType.DMA((2 + PIECES,)),
        ],
        compiler_params=pltpu.CompilerParams(vmem_limit_bytes=INTERP_LIMIT),
        cost_estimate=FREE,
        name="interp",
    )(slot, src, interp)


def load_body(levels, whole, table_hbm, *rest):
    sems = rest[-1]
    loaded = rest[whole + 1 : -1]
    sources = [table_hbm.at[level] for level in levels] + list(rest[:whole])
    loads = [
        pltpu.make_async_copy(source, target, sems.at[i])
        for i, (source, target) in enumerate(zip(sources, loaded))
    ]
    for copy in loads:
        copy.start()
    for copy in loads:
        copy.wait()


def load_call(levels, tables, whole, after, passes=False):
    outs = [jax.ShapeDtypeStruct(tables.shape[1:], tables.dtype)] * len(levels)
    outs += [jax.ShapeDtypeStruct(array.shape, array.dtype) for array in whole]
    count = len(outs)
    specs = [pl.BlockSpec(memory_space=pltpu.VMEM)] * count
    if passes:
        outs.append(jax.ShapeDtypeStruct(after.shape, after.dtype))
        specs.append(pl.BlockSpec(memory_space=pl.ANY))
    return pl.pallas_call(
        functools.partial(load_body, levels, len(whole)),
        in_specs=[pl.BlockSpec(memory_space=pl.ANY)] * (2 + len(whole)),
        out_specs=specs,
        out_shape=outs,
        input_output_aliases={1 + len(whole): count} if passes else {},
        scratch_shapes=[pltpu.SemaphoreType.DMA((count,))],
        compiler_params=pltpu.CompilerParams(vmem_limit_bytes=LOAD_LIMIT),
        cost_estimate=FREE,
        name="load",
    )(tables, *whole, after)


def level_body(first, parts, table_ref, own_ref, *rest):
    out_ref = rest[-1]
    far_refs = rest[:parts]
    _, rank, both = table_ref.shape
    groups, _, lanes = own_ref.shape
    for grp in range(groups):
        at = (first + grp) * PACK
        block = table_ref[at : at + PACK].reshape(PACK * rank, both)
        per = groups // parts
        pair = jnp.concatenate([own_ref[grp], far_refs[grp // per][grp % per]], axis=0)
        wide = jnp.dot(block, pair, preferred_element_type=jnp.float32)
        out_ref[grp] = pick(wide, rank, lanes // PACK).astype(jnp.bfloat16)


def level_call(first, table, own, fars, *after):
    groups, rank, lanes = own.shape
    both = table.shape[2]
    return pl.pallas_call(
        functools.partial(level_body, first, len(fars)),
        in_specs=[pl.BlockSpec(memory_space=pltpu.VMEM)] * (2 + len(fars))
        + [pl.BlockSpec(memory_space=pl.ANY)] * len(after),
        out_specs=pl.BlockSpec(memory_space=pltpu.VMEM),
        out_shape=jax.ShapeDtypeStruct(own.shape, jnp.bfloat16),
        compiler_params=pltpu.CompilerParams(vmem_limit_bytes=VMEM_LIMIT),
        cost_estimate=FREE,
        name="level",
    )(table, own, *fars, *after)


def eval_body(first, place_of, coeffs_ref, eval_ref, *rest):
    out_ref = rest[-1]
    _, rank, span = eval_ref.shape
    groups, _, lanes = coeffs_ref.shape
    rhs = lanes // PACK
    for grp in range(groups):
        mine = coeffs_ref[grp].astype(jnp.float32)
        twice = jnp.concatenate([mine, mine], axis=0).T.astype(jnp.bfloat16)
        left = jnp.concatenate([twice] * (PACK // 2), axis=1)
        row_box = lax.broadcasted_iota(jnp.int32, left.shape, 0) // rhs
        col_box = lax.broadcasted_iota(jnp.int32, left.shape, 1) // rank
        left = jnp.where(row_box == col_box, left, jnp.zeros_like(left))
        at = (first + grp) * PACK
        block = eval_ref[at : at + PACK].reshape(PACK * rank, span)
        vals = jnp.dot(left, block, preferred_element_type=jnp.float32)
        for box in range(PACK):
            mine = vals[box * rhs : (box + 1) * rhs]
            out_ref[place_of[at + box]] = mine.astype(jnp.bfloat16)


def eval_call(first, place_of, coeffs, evaluate, *before):
    groups, rank, lanes = coeffs.shape
    boxes, _, span = evaluate.shape
    rhs = lanes // PACK
    return pl.pallas_call(
        functools.partial(eval_body, first, place_of),
        in_specs=[pl.BlockSpec(memory_space=pltpu.VMEM)] * (2 + len(before)),
        out_specs=pl.BlockSpec(memory_space=pltpu.VMEM),
        out_shape=jax.ShapeDtypeStruct((boxes, rhs, span), jnp.bfloat16),
        input_output_aliases={2: 0} if before else {},
        compiler_params=pltpu.CompilerParams(vmem_limit_bytes=VMEM_LIMIT),
        cost_estimate=EVALUATE_COST,
        name="evaluate",
    )(coeffs, evaluate, *before)


def bits_by_shift():
    widths = [size.bit_length() - 1 for size in SPLIT]
    old = {axis: sum(widths[axis + 1 :]) for axis in range(len(SPLIT))}
    masks = {}
    for at, axis in enumerate(ORDER):
        new = sum(widths[later] for later in ORDER[at + 1 :])
        shift = new - old[axis]
        masks[shift] = masks.get(shift, 0) | (SPLIT[axis] - 1) << new
    return sorted(masks.items())


def place_of_device(device):
    place = 0
    for shift, mask in bits_by_shift():
        moved = device << shift if shift >= 0 else device >> -shift
        place = place | (moved & mask)
    return place


def place_body(pieces, slot_ref, got_ref, *rest):
    out_hbm, out_ref, sems = rest[-3:]
    boxes, _, span = got_ref.shape
    per = boxes // pieces
    stores = []
    for piece in range(pieces):
        for box in range(piece * per, (piece + 1) * per):
            out_ref[:, box * span : (box + 1) * span] = got_ref[place_of_device(slot_ref[box])]
        at = pl.ds(piece * per * span, per * span)
        stores.append(
            pltpu.make_async_copy(out_ref.at[:, at], out_hbm.at[:, at], sems.at[piece])
        )
        stores[-1].start()
    for store in stores:
        store.wait()


def place_call(slot, got):
    pieces = 4
    boxes, rhs, span = got.shape
    shape = (rhs, boxes * span)
    return pl.pallas_call(
        functools.partial(place_body, pieces),
        in_specs=[
            pl.BlockSpec(memory_space=pltpu.SMEM),
            pl.BlockSpec(memory_space=pltpu.VMEM),
        ],
        out_specs=pl.BlockSpec(memory_space=pl.ANY),
        out_shape=jax.ShapeDtypeStruct(shape, got.dtype),
        scratch_shapes=[
            pltpu.VMEM(shape, got.dtype),
            pltpu.SemaphoreType.DMA((pieces,)),
        ],
        compiler_params=pltpu.CompilerParams(vmem_limit_bytes=VMEM_LIMIT),
        cost_estimate=FREE,
        name="place",
    )(slot, got)


def from_partner(value, axis, distance):
    mask = 2**distance
    pairs = [(source, source ^ mask) for source in range(lax.axis_size(axis))]
    return lax.ppermute(value, axis, pairs)


def kernel_order(steps, chunks):
    order, at = [], 0
    while at < len(steps):
        width = 2 if at + 1 < len(steps) and steps[at + 1] == CORE_STEP else 1
        for i in range(chunks):
            order += [(level, i) for level in range(at, at + width)]
        at += width
    return order


def local(sources, in_slot, interp, translate, evaluate, owner_slot):
    firsts = [sum(CHUNKS[:i]) for i in range(len(CHUNKS))]
    coeffs = list(interp_call(firsts, in_slot, sources, interp))
    steps = [
        (axis, bit_pos)
        for axis in ("gz", "gy", "gx")
        for bit_pos in range(lax.axis_size(axis).bit_length() - 1)
    ]
    tables = {}
    *held, coeffs[-1] = load_call(range(EARLY), translate, [], coeffs[-1], True)
    last = coeffs[-1]
    for level, i in kernel_order(steps, len(firsts)):
        axis, bit_pos = steps[level]
        if i == 0:
            more = ()
            if level in LOADS:
                levels = range(len(held), len(held) + LOADS[level])
                final = level == len(steps) - 1
                more = load_call(levels, translate, [evaluate] * final, coeffs[-1])
                held += more[: len(levels)]
                if final:
                    evaluate = more[-1]
            tables[level] = more[:1]
        parts = CORE_PARTS if steps[level] == CORE_STEP else 1
        pieces = jnp.split(coeffs[i], parts) if parts > 1 else [coeffs[i]]
        fars = [from_partner(piece, axis, bit_pos) for piece in pieces]
        last = coeffs[i] = level_call(
            firsts[i], held[level], coeffs[i], fars, last, *tables[level]
        )
    devices = np.arange(int(np.prod(SPLIT))).reshape(SPLIT).transpose(ORDER).reshape(-1)
    group = [int(device) for device in devices]
    place_of = [int(at) for at in np.argsort(devices)]
    values = ()
    for i, first in enumerate(firsts):
        values = (eval_call(first, place_of, coeffs[i], evaluate, *values),)
    moved = lax.all_to_all(
        values[0], AXES, split_axis=0, concat_axis=0, axis_index_groups=[group], tiled=True
    )
    return place_call(owner_slot, moved)


def solution(mesh):
    placed = (
        P(None, AXES),
        P(AXES),
        P(AXES, None, None),
        P(None, AXES, None, None),
        P(AXES, None, None),
        P(AXES),
    )
    return jax.shard_map(
        local, mesh=mesh, in_specs=placed, out_specs=P(None, AXES), check_vma=False
    )
```

```python
import functools

import jax
import jax.numpy as jnp
import numpy as np
from jax import lax
from jax.experimental import pallas as pl
from jax.experimental.pallas import tpu as pltpu
from jax.sharding import PartitionSpec as P

AXES = ("gx", "gy", "gz")
PACK = 8
CHUNKS = (8, 8)
EARLY = 1
LOADS = {0: 1, 1: 1, 2: 1, 3: 2, 6: 1}
PIECES = 4
ORDER = (1, 2, 3, 0, 4)
SPLIT = (2, 2, 4, 2, 4)
CORE_STEP = ("gx", 0)
CORE_PARTS = 2
EVALUATE_COST = pl.CostEstimate(flops=10**9, bytes_accessed=0, transcendentals=0)
MIB = 2**20
FREE = pl.CostEstimate(flops=0, bytes_accessed=0, transcendentals=0)
VMEM_LIMIT = 16 * MIB
INTERP_LIMIT = int(53.25 * MIB)
LOAD_LIMIT = 38 * MIB


def own_lanes(shape, cols):
    return lax.broadcasted_iota(jnp.int32, shape, 1) // cols


def pick(wide, rank, cols):
    lane_box = own_lanes((rank, PACK * cols), cols)
    out = wide[:rank]
    for box in range(1, PACK):
        out = jnp.where(lane_box == box, wide[box * rank : (box + 1) * rank], out)
    return out


def interp_body(firsts, slot_hbm, src_hbm, interp_hbm, *rest):
    *out_refs, slot_ref, src_ref, interp_ref, sems = rest
    boxes, rank, span = interp_ref.shape
    rhs = src_ref.shape[0]
    per = boxes // PIECES
    ready = [
        pltpu.make_async_copy(slot_hbm, slot_ref, sems.at[0]),
        pltpu.make_async_copy(src_hbm, src_ref, sems.at[1]),
    ]
    loads = []
    for piece in range(PIECES):
        at = pl.ds(piece * per, per)
        loads.append(
            pltpu.make_async_copy(interp_hbm.at[at], interp_ref.at[at], sems.at[2 + piece])
        )
    for copy in ready + loads:
        copy.start()
    for copy in ready:
        copy.wait()
    for first, out_ref in zip(firsts, out_refs):
        for grp in range(out_ref.shape[0]):
            base = (first + grp) * PACK
            slabs = []
            for box in range(PACK):
                at = pl.multiple_of(slot_ref[base + box] * span, span)
                slabs.append(src_ref[:, pl.ds(at, span)])
            inputs = jnp.concatenate(slabs, axis=0)
            if base % per == 0:
                loads[base // per].wait()
            block = interp_ref[base : base + PACK].reshape(PACK * rank, span)
            wide = lax.dot_general(
                block, inputs, (((1,), (1,)), ((), ())), preferred_element_type=jnp.float32
            )
            out_ref[grp] = pick(wide, rank, rhs).astype(jnp.bfloat16)


def interp_call(firsts, slot, src, interp):
    _, rank, span = interp.shape
    lanes = PACK * src.shape[0]
    return pl.pallas_call(
        functools.partial(interp_body, firsts),
        in_specs=[pl.BlockSpec(memory_space=pl.ANY)] * 3,
        out_specs=[pl.BlockSpec(memory_space=pltpu.VMEM)] * len(firsts),
        out_shape=[
            jax.ShapeDtypeStruct((groups, rank, lanes), jnp.bfloat16) for groups in CHUNKS
        ],
        scratch_shapes=[
            pltpu.SMEM(slot.shape, slot.dtype),
            pltpu.VMEM(src.shape, src.dtype),
            pltpu.VMEM(interp.shape, interp.dtype),
            pltpu.SemaphoreType.DMA((2 + PIECES,)),
        ],
        compiler_params=pltpu.CompilerParams(vmem_limit_bytes=INTERP_LIMIT),
        cost_estimate=FREE,
        name="interp",
    )(slot, src, interp)


def load_body(levels, whole, table_hbm, *rest):
    sems = rest[-1]
    loaded = rest[whole + 1 : -1]
    sources = [table_hbm.at[level] for level in levels] + list(rest[:whole])
    loads = [
        pltpu.make_async_copy(source, target, sems.at[i])
        for i, (source, target) in enumerate(zip(sources, loaded))
    ]
    for copy in loads:
        copy.start()
    for copy in loads:
        copy.wait()


def load_call(levels, tables, whole, after, passes=False):
    outs = [jax.ShapeDtypeStruct(tables.shape[1:], tables.dtype)] * len(levels)
    outs += [jax.ShapeDtypeStruct(array.shape, array.dtype) for array in whole]
    count = len(outs)
    specs = [pl.BlockSpec(memory_space=pltpu.VMEM)] * count
    if passes:
        outs.append(jax.ShapeDtypeStruct(after.shape, after.dtype))
        specs.append(pl.BlockSpec(memory_space=pl.ANY))
    return pl.pallas_call(
        functools.partial(load_body, levels, len(whole)),
        in_specs=[pl.BlockSpec(memory_space=pl.ANY)] * (2 + len(whole)),
        out_specs=specs,
        out_shape=outs,
        input_output_aliases={1 + len(whole): count} if passes else {},
        scratch_shapes=[pltpu.SemaphoreType.DMA((count,))],
        compiler_params=pltpu.CompilerParams(vmem_limit_bytes=LOAD_LIMIT),
        cost_estimate=FREE,
        name="load",
    )(tables, *whole, after)


def level_body(first, parts, table_ref, own_ref, *rest):
    out_ref = rest[-1]
    far_refs = rest[:parts]
    _, rank, both = table_ref.shape
    groups, _, lanes = own_ref.shape
    for grp in range(groups):
        at = (first + grp) * PACK
        block = table_ref[at : at + PACK].reshape(PACK * rank, both)
        per = groups // parts
        pair = jnp.concatenate([own_ref[grp], far_refs[grp // per][grp % per]], axis=0)
        wide = jnp.dot(block, pair, preferred_element_type=jnp.float32)
        out_ref[grp] = pick(wide, rank, lanes // PACK).astype(jnp.bfloat16)


def level_call(first, table, own, fars, *after):
    groups, rank, lanes = own.shape
    both = table.shape[2]
    return pl.pallas_call(
        functools.partial(level_body, first, len(fars)),
        in_specs=[pl.BlockSpec(memory_space=pltpu.VMEM)] * (2 + len(fars))
        + [pl.BlockSpec(memory_space=pl.ANY)] * len(after),
        out_specs=pl.BlockSpec(memory_space=pltpu.VMEM),
        out_shape=jax.ShapeDtypeStruct(own.shape, jnp.bfloat16),
        compiler_params=pltpu.CompilerParams(vmem_limit_bytes=VMEM_LIMIT),
        cost_estimate=FREE,
        name="level",
    )(table, own, *fars, *after)


def last_body(first, place_of, table_ref, own_ref, far_ref, eval_ref, *rest):
    out_ref = rest[-1]
    _, rank, both = table_ref.shape
    span = eval_ref.shape[2]
    groups, _, lanes = own_ref.shape
    rhs = lanes // PACK
    for grp in range(groups):
        at = (first + grp) * PACK
        block = table_ref[at : at + PACK].reshape(PACK * rank, both)
        pair = jnp.concatenate([own_ref[grp], far_ref[grp]], axis=0)
        wide = jnp.dot(block, pair, preferred_element_type=jnp.float32)
        mine = pick(wide, rank, rhs).astype(jnp.bfloat16).astype(jnp.float32)
        twice = jnp.concatenate([mine, mine], axis=0).T.astype(jnp.bfloat16)
        left = jnp.concatenate([twice] * (PACK // 2), axis=1)
        row_box = lax.broadcasted_iota(jnp.int32, left.shape, 0) // rhs
        col_box = lax.broadcasted_iota(jnp.int32, left.shape, 1) // rank
        left = jnp.where(row_box == col_box, left, jnp.zeros_like(left))
        block = eval_ref[at : at + PACK].reshape(PACK * rank, span)
        vals = jnp.dot(left, block, preferred_element_type=jnp.float32)
        for box in range(PACK):
            own = vals[box * rhs : (box + 1) * rhs]
            out_ref[place_of[at + box]] = own.astype(jnp.bfloat16)


def last_call(first, place_of, table, own, far, evaluate, *before):
    boxes, _, span = evaluate.shape
    rhs = own.shape[2] // PACK
    return pl.pallas_call(
        functools.partial(last_body, first, place_of),
        in_specs=[pl.BlockSpec(memory_space=pltpu.VMEM)] * (4 + len(before)),
        out_specs=pl.BlockSpec(memory_space=pltpu.VMEM),
        out_shape=jax.ShapeDtypeStruct((boxes, rhs, span), jnp.bfloat16),
        input_output_aliases={4: 0} if before else {},
        compiler_params=pltpu.CompilerParams(vmem_limit_bytes=VMEM_LIMIT),
        cost_estimate=EVALUATE_COST,
        name="last",
    )(table, own, far, evaluate, *before)


def bits_by_shift():
    widths = [size.bit_length() - 1 for size in SPLIT]
    old = {axis: sum(widths[axis + 1 :]) for axis in range(len(SPLIT))}
    masks = {}
    for at, axis in enumerate(ORDER):
        new = sum(widths[later] for later in ORDER[at + 1 :])
        shift = new - old[axis]
        masks[shift] = masks.get(shift, 0) | (SPLIT[axis] - 1) << new
    return sorted(masks.items())


def place_of_device(device):
    place = 0
    for shift, mask in bits_by_shift():
        moved = device << shift if shift >= 0 else device >> -shift
        place = place | (moved & mask)
    return place


def place_body(pieces, slot_ref, got_ref, *rest):
    out_hbm, out_ref, sems = rest[-3:]
    boxes, _, span = got_ref.shape
    per = boxes // pieces
    stores = []
    for piece in range(pieces):
        for box in range(piece * per, (piece + 1) * per):
            out_ref[:, box * span : (box + 1) * span] = got_ref[place_of_device(slot_ref[box])]
        at = pl.ds(piece * per * span, per * span)
        stores.append(
            pltpu.make_async_copy(out_ref.at[:, at], out_hbm.at[:, at], sems.at[piece])
        )
        stores[-1].start()
    for store in stores:
        store.wait()


def place_call(slot, got):
    pieces = 8
    boxes, rhs, span = got.shape
    shape = (rhs, boxes * span)
    return pl.pallas_call(
        functools.partial(place_body, pieces),
        in_specs=[
            pl.BlockSpec(memory_space=pltpu.SMEM),
            pl.BlockSpec(memory_space=pltpu.VMEM),
        ],
        out_specs=pl.BlockSpec(memory_space=pl.ANY),
        out_shape=jax.ShapeDtypeStruct(shape, got.dtype),
        scratch_shapes=[
            pltpu.VMEM(shape, got.dtype),
            pltpu.SemaphoreType.DMA((pieces,)),
        ],
        compiler_params=pltpu.CompilerParams(vmem_limit_bytes=VMEM_LIMIT),
        cost_estimate=FREE,
        name="place",
    )(slot, got)


def from_partner(value, axis, distance):
    mask = 2**distance
    pairs = [(source, source ^ mask) for source in range(lax.axis_size(axis))]
    return lax.ppermute(value, axis, pairs)


def kernel_order(steps, chunks):
    order, at = [], 0
    while at < len(steps):
        width = 2 if at + 1 < len(steps) and steps[at + 1] == CORE_STEP else 1
        for i in range(chunks):
            order += [(level, i) for level in range(at, at + width)]
        at += width
    return order


def local(sources, in_slot, interp, translate, evaluate, owner_slot):
    firsts = [sum(CHUNKS[:i]) for i in range(len(CHUNKS))]
    coeffs = list(interp_call(firsts, in_slot, sources, interp))
    steps = [
        (axis, bit_pos)
        for axis in ("gz", "gy", "gx")
        for bit_pos in range(lax.axis_size(axis).bit_length() - 1)
    ]
    devices = np.arange(int(np.prod(SPLIT))).reshape(SPLIT).transpose(ORDER).reshape(-1)
    group = [int(device) for device in devices]
    place_of = [int(at) for at in np.argsort(devices)]
    values = ()
    tables = {}
    *held, coeffs[-1] = load_call(range(EARLY), translate, [], coeffs[-1], True)
    last = coeffs[-1]
    for level, i in kernel_order(steps, len(firsts)):
        axis, bit_pos = steps[level]
        if i == 0:
            more = ()
            if level in LOADS:
                levels = range(len(held), len(held) + LOADS[level])
                final = level == len(steps) - 1
                more = load_call(levels, translate, [evaluate] * final, coeffs[-1])
                held += more[: len(levels)]
                if final:
                    evaluate = more[-1]
            tables[level] = more[:1]
        parts = CORE_PARTS if steps[level] == CORE_STEP else 1
        pieces = jnp.split(coeffs[i], parts) if parts > 1 else [coeffs[i]]
        fars = [from_partner(piece, axis, bit_pos) for piece in pieces]
        if level == len(steps) - 1:
            values = (
                last_call(firsts[i], place_of, held[level], coeffs[i], fars[0], evaluate, *values),
            )
            continue
        last = coeffs[i] = level_call(
            firsts[i], held[level], coeffs[i], fars, last, *tables[level]
        )
    moved = lax.all_to_all(
        values[0], AXES, split_axis=0, concat_axis=0, axis_index_groups=[group], tiled=True
    )
    return place_call(owner_slot, moved)


def solution(mesh):
    placed = (
        P(None, AXES),
        P(AXES),
        P(AXES, None, None),
        P(None, AXES, None, None),
        P(AXES, None, None),
        P(AXES),
    )
    return jax.shard_map(
        local, mesh=mesh, in_specs=placed, out_specs=P(None, AXES), check_vma=False
    )
```

```python
import functools

import jax
import jax.numpy as jnp
import numpy as np
from jax import lax
from jax.experimental import pallas as pl
from jax.experimental.pallas import tpu as pltpu
from jax.sharding import PartitionSpec as P

AXES = ("gx", "gy", "gz")
PACK = 8
CHUNKS = (8, 8)
EARLY = 1
LOADS = {0: 1, 1: 1, 2: 1, 3: 2, 6: 1}
PIECES = 4
ORDER = (1, 2, 3, 0, 4)
SPLIT = (2, 2, 4, 2, 4)
CORE_STEP = ("gx", 0)
CORE_PARTS = 2
EVALUATE_COST = pl.CostEstimate(flops=10**9, bytes_accessed=0, transcendentals=0)
MIB = 2**20
FREE = pl.CostEstimate(flops=0, bytes_accessed=0, transcendentals=0)
VMEM_LIMIT = 16 * MIB
INTERP_LIMIT = int(53.25 * MIB)
LOAD_LIMIT = 38 * MIB


def own_lanes(shape, cols):
    return lax.broadcasted_iota(jnp.int32, shape, 1) // cols


def pick(wide, rank, cols):
    lane_box = own_lanes((rank, PACK * cols), cols)
    out = wide[:rank]
    for box in range(1, PACK):
        out = jnp.where(lane_box == box, wide[box * rank : (box + 1) * rank], out)
    return out


def interp_body(firsts, slot_hbm, src_hbm, interp_hbm, *rest):
    *out_refs, slot_ref, src_ref, interp_ref, sems = rest
    boxes, rank, span = interp_ref.shape
    rhs = src_ref.shape[0]
    per = boxes // PIECES
    ready = [
        pltpu.make_async_copy(slot_hbm, slot_ref, sems.at[0]),
        pltpu.make_async_copy(src_hbm, src_ref, sems.at[1]),
    ]
    loads = []
    for piece in range(PIECES):
        at = pl.ds(piece * per, per)
        loads.append(
            pltpu.make_async_copy(interp_hbm.at[at], interp_ref.at[at], sems.at[2 + piece])
        )
    for copy in ready + loads:
        copy.start()
    for copy in ready:
        copy.wait()
    for first, out_ref in zip(firsts, out_refs):
        for grp in range(out_ref.shape[0]):
            base = (first + grp) * PACK
            slabs = []
            for box in range(PACK):
                at = pl.multiple_of(slot_ref[base + box] * span, span)
                slabs.append(src_ref[:, pl.ds(at, span)])
            inputs = jnp.concatenate(slabs, axis=0)
            if base % per == 0:
                loads[base // per].wait()
            block = interp_ref[base : base + PACK].reshape(PACK * rank, span)
            wide = lax.dot_general(
                block, inputs, (((1,), (1,)), ((), ())), preferred_element_type=jnp.float32
            )
            out_ref[grp] = pick(wide, rank, rhs).astype(jnp.bfloat16)


def interp_call(firsts, slot, src, interp):
    _, rank, span = interp.shape
    lanes = PACK * src.shape[0]
    return pl.pallas_call(
        functools.partial(interp_body, firsts),
        in_specs=[pl.BlockSpec(memory_space=pl.ANY)] * 3,
        out_specs=[pl.BlockSpec(memory_space=pltpu.VMEM)] * len(firsts),
        out_shape=[
            jax.ShapeDtypeStruct((groups, rank, lanes), jnp.bfloat16) for groups in CHUNKS
        ],
        scratch_shapes=[
            pltpu.SMEM(slot.shape, slot.dtype),
            pltpu.VMEM(src.shape, src.dtype),
            pltpu.VMEM(interp.shape, interp.dtype),
            pltpu.SemaphoreType.DMA((2 + PIECES,)),
        ],
        compiler_params=pltpu.CompilerParams(vmem_limit_bytes=INTERP_LIMIT),
        cost_estimate=FREE,
        name="interp",
    )(slot, src, interp)


def load_body(levels, whole, table_hbm, *rest):
    sems = rest[-1]
    loaded = rest[whole + 1 : -1]
    sources = [table_hbm.at[level] for level in levels] + list(rest[:whole])
    loads = [
        pltpu.make_async_copy(source, target, sems.at[i])
        for i, (source, target) in enumerate(zip(sources, loaded))
    ]
    for copy in loads:
        copy.start()
    for copy in loads:
        copy.wait()


def load_call(levels, tables, whole, after, passes=False):
    outs = [jax.ShapeDtypeStruct(tables.shape[1:], tables.dtype)] * len(levels)
    outs += [jax.ShapeDtypeStruct(array.shape, array.dtype) for array in whole]
    count = len(outs)
    specs = [pl.BlockSpec(memory_space=pltpu.VMEM)] * count
    if passes:
        outs.append(jax.ShapeDtypeStruct(after.shape, after.dtype))
        specs.append(pl.BlockSpec(memory_space=pl.ANY))
    return pl.pallas_call(
        functools.partial(load_body, levels, len(whole)),
        in_specs=[pl.BlockSpec(memory_space=pl.ANY)] * (2 + len(whole)),
        out_specs=specs,
        out_shape=outs,
        input_output_aliases={1 + len(whole): count} if passes else {},
        scratch_shapes=[pltpu.SemaphoreType.DMA((count,))],
        compiler_params=pltpu.CompilerParams(vmem_limit_bytes=LOAD_LIMIT),
        cost_estimate=FREE,
        name="load",
    )(tables, *whole, after)


def level_body(first, parts, table_ref, own_ref, *rest):
    out_ref = rest[-1]
    far_refs = rest[:parts]
    _, rank, both = table_ref.shape
    groups, _, lanes = own_ref.shape
    for grp in range(groups):
        at = (first + grp) * PACK
        block = table_ref[at : at + PACK].reshape(PACK * rank, both)
        per = groups // parts
        pair = jnp.concatenate([own_ref[grp], far_refs[grp // per][grp % per]], axis=0)
        wide = jnp.dot(block, pair, preferred_element_type=jnp.float32)
        out_ref[grp] = pick(wide, rank, lanes // PACK).astype(jnp.bfloat16)


def level_call(first, table, own, fars, *after):
    groups, rank, lanes = own.shape
    both = table.shape[2]
    return pl.pallas_call(
        functools.partial(level_body, first, len(fars)),
        in_specs=[pl.BlockSpec(memory_space=pltpu.VMEM)] * (2 + len(fars))
        + [pl.BlockSpec(memory_space=pl.ANY)] * len(after),
        out_specs=pl.BlockSpec(memory_space=pltpu.VMEM),
        out_shape=jax.ShapeDtypeStruct(own.shape, jnp.bfloat16),
        compiler_params=pltpu.CompilerParams(vmem_limit_bytes=VMEM_LIMIT),
        cost_estimate=FREE,
        name="level",
    )(table, own, *fars, *after)


def last_body(first, place_of, table_ref, own_ref, far_ref, eval_ref, *rest):
    out_ref = rest[-1]
    _, rank, both = table_ref.shape
    span = eval_ref.shape[2]
    groups, _, lanes = own_ref.shape
    rhs = lanes // PACK
    for grp in range(groups):
        at = (first + grp) * PACK
        block = table_ref[at : at + PACK].reshape(PACK * rank, both)
        pair = jnp.concatenate([own_ref[grp], far_ref[grp]], axis=0)
        wide = jnp.dot(block, pair, preferred_element_type=jnp.float32)
        mine = pick(wide, rank, rhs).astype(jnp.bfloat16).astype(jnp.float32)
        twice = jnp.concatenate([mine, mine], axis=0).T.astype(jnp.bfloat16)
        left = jnp.concatenate([twice] * (PACK // 2), axis=1)
        row_box = lax.broadcasted_iota(jnp.int32, left.shape, 0) // rhs
        col_box = lax.broadcasted_iota(jnp.int32, left.shape, 1) // rank
        left = jnp.where(row_box == col_box, left, jnp.zeros_like(left))
        block = eval_ref[at : at + PACK].reshape(PACK * rank, span)
        vals = jnp.dot(left, block, preferred_element_type=jnp.float32)
        for box in range(PACK):
            own = vals[box * rhs : (box + 1) * rhs]
            out_ref[place_of[at + box]] = own.astype(jnp.bfloat16)


def last_call(first, place_of, table, own, far, evaluate, *before):
    boxes, _, span = evaluate.shape
    rhs = own.shape[2] // PACK
    return pl.pallas_call(
        functools.partial(last_body, first, place_of),
        in_specs=[pl.BlockSpec(memory_space=pltpu.VMEM)] * (4 + len(before)),
        out_specs=pl.BlockSpec(memory_space=pltpu.VMEM),
        out_shape=jax.ShapeDtypeStruct((boxes, rhs, span), jnp.bfloat16),
        input_output_aliases={4: 0} if before else {},
        compiler_params=pltpu.CompilerParams(vmem_limit_bytes=VMEM_LIMIT),
        cost_estimate=EVALUATE_COST,
        name="last",
    )(table, own, far, evaluate, *before)


def bits_by_shift():
    widths = [size.bit_length() - 1 for size in SPLIT]
    old = {axis: sum(widths[axis + 1 :]) for axis in range(len(SPLIT))}
    masks = {}
    for at, axis in enumerate(ORDER):
        new = sum(widths[later] for later in ORDER[at + 1 :])
        shift = new - old[axis]
        masks[shift] = masks.get(shift, 0) | (SPLIT[axis] - 1) << new
    return sorted(masks.items())


def place_of_device(device):
    place = 0
    for shift, mask in bits_by_shift():
        moved = device << shift if shift >= 0 else device >> -shift
        place = place | (moved & mask)
    return place


def place_body(pieces, slot_ref, got_ref, *rest):
    out_hbm, out_ref, sems = rest[-3:]
    boxes, _, span = got_ref.shape
    per = boxes // pieces
    stores = []
    for piece in range(pieces):
        for box in range(piece * per, (piece + 1) * per):
            out_ref[:, box * span : (box + 1) * span] = got_ref[place_of_device(slot_ref[box])]
        at = pl.ds(piece * per * span, per * span)
        stores.append(
            pltpu.make_async_copy(out_ref.at[:, at], out_hbm.at[:, at], sems.at[piece])
        )
        stores[-1].start()
    for store in stores:
        store.wait()


def place_call(slot, got):
    pieces = 8
    boxes, rhs, span = got.shape
    shape = (rhs, boxes * span)
    return pl.pallas_call(
        functools.partial(place_body, pieces),
        in_specs=[
            pl.BlockSpec(memory_space=pltpu.SMEM),
            pl.BlockSpec(memory_space=pltpu.VMEM),
        ],
        out_specs=pl.BlockSpec(memory_space=pl.ANY),
        out_shape=jax.ShapeDtypeStruct(shape, got.dtype),
        scratch_shapes=[
            pltpu.VMEM(shape, got.dtype),
            pltpu.SemaphoreType.DMA((pieces,)),
        ],
        compiler_params=pltpu.CompilerParams(vmem_limit_bytes=VMEM_LIMIT),
        cost_estimate=FREE,
        name="place",
    )(slot, got)


def from_partner(value, axis, distance):
    mask = 2**distance
    pairs = [(source, source ^ mask) for source in range(lax.axis_size(axis))]
    return lax.ppermute(value, axis, pairs)


def kernel_order(steps, chunks):
    order, at = [], 0
    while at < len(steps):
        width = 2 if at + 1 < len(steps) and steps[at + 1] == CORE_STEP else 1
        for i in range(chunks):
            order += [(level, i) for level in range(at, at + width)]
        at += width
    return order


def local(sources, in_slot, interp, translate, evaluate, owner_slot):
    firsts = [sum(CHUNKS[:i]) for i in range(len(CHUNKS))]
    coeffs = list(interp_call(firsts, in_slot, sources, interp))
    steps = [
        (axis, bit_pos)
        for axis in ("gz", "gy", "gx")
        for bit_pos in range(lax.axis_size(axis).bit_length() - 1)
    ]
    devices = np.arange(int(np.prod(SPLIT))).reshape(SPLIT).transpose(ORDER).reshape(-1)
    group = [int(device) for device in devices]
    place_of = [int(at) for at in np.argsort(devices)]
    values = ()
    tables = {}
    *held, coeffs[-1] = load_call(range(EARLY), translate, [], coeffs[-1], True)
    last = coeffs[-1]
    for level, i in kernel_order(steps, len(firsts)):
        axis, bit_pos = steps[level]
        if i == 0:
            more = ()
            if level in LOADS:
                levels = range(len(held), len(held) + LOADS[level])
                more = load_call(levels, translate, [], coeffs[-1])
                held += more[: len(levels)]
            tables[level] = more[:1]
        parts = CORE_PARTS if steps[level] == CORE_STEP else 1
        pieces = jnp.split(coeffs[i], parts) if parts > 1 else [coeffs[i]]
        fars = [from_partner(piece, axis, bit_pos) for piece in pieces]
        if level == len(steps) - 1:
            values = (
                last_call(firsts[i], place_of, held[level], coeffs[i], fars[0], evaluate, *values),
            )
            continue
        last = coeffs[i] = level_call(
            firsts[i], held[level], coeffs[i], fars, last, *tables[level]
        )
    moved = lax.all_to_all(
        values[0], AXES, split_axis=0, concat_axis=0, axis_index_groups=[group], tiled=True
    )
    return place_call(owner_slot, moved)


def solution(mesh):
    placed = (
        P(None, AXES),
        P(AXES),
        P(AXES, None, None),
        P(None, AXES, None, None),
        P(AXES, None, None),
        P(AXES),
    )
    return jax.shard_map(
        local, mesh=mesh, in_specs=placed, out_specs=P(None, AXES), check_vma=False
    )
```
